128 devices in a mesh: dp: 8 (over z_lo, y), mp: 16 (over x, z_hi, core).
Axes of the slice: x: 4, y: 4, z: 4 (z_hi: 2, z_lo: 2; z = z_hi * 2 + z_lo), core: 2. Of those that a mesh axis runs over, the one named last changes fastest.
Arguments:
- inputs: bfloat16 [3072, 6144], P(('dp', 'mp')), may hold values from -24 to 24
- out_grad: bfloat16 [3072, 6144], P(('dp', 'mp')), may hold values from -24 to 24
- hidden_pre: bfloat16 [3072, 12288], P('dp', 'mp'), may hold values from -8 to 8
- w_in: bfloat16 [6144, 12288], P(None, 'mp'), may hold values from -0.078125 to 0.078125
- w_out: bfloat16 [12288, 6144], P('mp'), may hold values from -0.0546875 to 0.0546875
Outputs:
- input_grad: bfloat16 [3072, 6144], P(('dp', 'mp'))
- in_weight_grad: float32 [6144, 12288], P('dp', 'mp')
- out_weight_grad: float32 [12288, 6144], P('mp', 'dp')
The draws below stay inside these ranges and needn't reach their ends.
All inputs are finite; a program needn't handle non-finite values.
Results may differ from the reference program's by a relative error of at most 0.019.
Values may be sent and summed in bfloat16 or wider, within the bound.
No kernel may reach another device: no remote copies, remote signals or barrier semaphores. Data moves between devices by JAX's collectives and lax.ppermute only.
A program may use at most 192 MiB of HBM per device.

```python
import math
import jax
import jax.numpy as jnp
from jax import lax

D = 6144
FF = 12288
ROW_DEV = 24
TOKENS = 3072
N_DP = 8
N_MP = 16


def strengthened(array, stream_key, source, target, shards_of, factor):
    def block_of(position):
        return (jnp.arange(array.shape[position]) // (array.shape[position] // shards_of)).reshape((-1,) + (1,) * (array.ndim - 1 - position))

    near = jax.random.permutation(stream_key, shards_of)[block_of(target)]
    second = (block_of(target) + shards_of // 2) % shards_of
    return jnp.where((block_of(source) == near) | (block_of(source) == second), factor * array, array)


def block_scale(stream_key, dims, shards, least, top_value):
    level = 1.0
    for position, shards_of in shards:
        steps = jax.random.uniform(jax.random.fold_in(jax.random.fold_in(stream_key, 6), position), (shards_of,), jnp.float32, least / len(shards), top_value / len(shards))
        level = level * jnp.repeat(jnp.exp(steps), dims[position] // shards_of).reshape((-1,) + (1,) * (len(dims) - 1 - position))
    return level


def gaussian(stream_key, shape, spread, most, split=(), held_as=jnp.bfloat16):
    loudness = block_scale(stream_key, shape, split, -0.22, 0.18) if split else 1.0
    array = jax.random.normal(stream_key, shape, jnp.float32) * spread * loudness
    return jnp.minimum(jnp.maximum(array, -most), most).astype(held_as)


def heavy_noise(own_key, dims, width, limit, split, heavy, kind=jnp.bfloat16):
    result = width * jax.random.normal(own_key, dims, jnp.float32)
    if split:
        result = result * block_scale(own_key, dims, split, -0.22, 0.18)
    return jnp.clip(strengthened(result, jax.random.fold_in(own_key, 3), *heavy), -limit, limit).astype(kind)


def setup_inputs(seed: int = 0) -> dict:
    splits = jax.random.split(jax.random.key(seed), 6)
    return {
        "inputs": heavy_noise(splits[0], (TOKENS, D), 1.0, 24.0, ((0, 128),), (0, 1, 128, 5.5)),
        "out_grad": heavy_noise(splits[1], (TOKENS, D), 1.0, 24.0, ((0, 128),), (0, 1, 128, 5.5)),
        "hidden_pre": gaussian(splits[2], (TOKENS, FF), 1.5, 8.0, ((0, 8), (1, 16))),
        "w_in": gaussian(splits[3], (D, FF), D ** -0.5, 0.078125, ((1, 16),)),
        "w_out": gaussian(splits[4], (FF, D), FF ** -0.5, 0.0546875, ((0, 16),)),
    }


root_two_pi = math.sqrt(2.0 / math.pi)
cubic_coef = 0.044715

def gelu_parts(pre):
    inner = root_two_pi * (pre + cubic_coef * pre * pre * pre)
    tanh_part = jnp.tanh(inner)
    value = 0.5 * pre * (1.0 + tanh_part)
    slope = 0.5 * (1.0 + tanh_part) + 0.5 * pre * (1.0 - tanh_part * tanh_part) * root_two_pi * (1.0 + 3.0 * cubic_coef * pre * pre)
    return (value, slope)

def reference(inputs, out_grad, hidden_pre, w_in, w_out):
    group = ROW_DEV * N_MP
    scale = jnp.float32(1.0 / math.sqrt(TOKENS))
    value, slope = gelu_parts(hidden_pre.astype(jnp.float32))
    activation = value.astype(jnp.bfloat16)
    act_grad = lax.dot_general(out_grad, w_out, (((1,), (1,)), ((), ())), preferred_element_type=jnp.float32)
    pre_grad = (act_grad * slope).astype(jnp.bfloat16)
    input_grad = lax.dot_general(pre_grad, w_in, (((1,), (1,)), ((), ())), preferred_element_type=jnp.float32).astype(jnp.bfloat16)
    blocks = (inputs.reshape(N_DP, group, D), out_grad.reshape(N_DP, group, D), activation.reshape(N_DP, group, FF), pre_grad.reshape(N_DP, group, FF))

    def per_block(carry, parts):
        in_rows, grad_rows, act_rows, pre_rows = parts
        out_term = lax.dot_general(act_rows, grad_rows, (((0,), (0,)), ((), ())), preferred_element_type=jnp.float32) * scale
        in_term = lax.dot_general(in_rows, pre_rows, (((0,), (0,)), ((), ())), preferred_element_type=jnp.float32) * scale
        out_term = lax.optimization_barrier(out_term.astype(jnp.bfloat16)).astype(jnp.float32)
        in_term = lax.optimization_barrier(in_term.astype(jnp.bfloat16)).astype(jnp.float32)
        return ((carry[0] + in_term, carry[1] + out_term), None)
    start_carry = (jnp.zeros((D, FF), jnp.float32), jnp.zeros((FF, D), jnp.float32))
    (in_weight_grad, out_weight_grad), unused = lax.scan(per_block, start_carry, blocks)
    return (input_grad, in_weight_grad, out_weight_grad)
```

```python
import math

import jax
import jax.numpy as jnp
from jax import lax
from jax.sharding import PartitionSpec as P

root_two_pi = math.sqrt(2.0 / math.pi)
cubic_coef = 0.044715
AXES = ("dp", "mp")
NX, NY = 4, 4
BF, F32 = jnp.bfloat16, jnp.float32


def gelu_parts(pre):
    inner = root_two_pi * (pre + cubic_coef * pre * pre * pre)
    tanh_part = jnp.tanh(inner)
    value = 0.5 * pre * (1.0 + tanh_part)
    slope = 0.5 * (1.0 + tanh_part) + 0.5 * pre * (1.0 - tanh_part * tanh_part) * root_two_pi * (
        1.0 + 3.0 * cubic_coef * pre * pre
    )
    return (value, slope)


def contract_rows(left, right):
    return lax.dot_general(left, right, (((0,), (0,)), ((), ())), preferred_element_type=F32)


def contract_last(left, right):
    return lax.dot_general(left, right, (((1,), (1,)), ((), ())), preferred_element_type=F32)


def number(zl, y, x, zh, c):
    return (zl * NY + y) * 16 + x * 4 + zh * 2 + c


def hop(array, dzl=0, dy=0, dx=0, dzh=0, dc=0):
    pairs = []
    for zl in range(2):
        for y in range(NY):
            for x in range(NX):
                for zh in range(2):
                    for c in range(2):
                        there = number(zl ^ dzl, (y + dy) % NY, (x + dx) % NX, zh ^ dzh, c ^ dc)
                        pairs.append((number(zl, y, x, zh, c), there))
    return lax.ppermute(array, AXES, pairs)


def over_x(first):
    right = hop(first, dx=-1)
    left = hop(first, dx=1)
    far_a = hop(right[0], dx=-1)
    far_b = hop(left[1], dx=1)
    return jnp.stack([first, right, jnp.stack([far_a, far_b]), left])


def per_device(inputs, out_grad, hidden_pre, w_in, w_out):
    own, width = out_grad.shape
    dp = lax.axis_index("dp")
    mp = lax.axis_index("mp")
    zl, y = dp // NY, dp % NY
    x, zh, c = mp // 4, (mp // 2) % 2, mp % 2
    cols = width // 8
    hid = hidden_pre.shape[1]
    scale = 1.0 / math.sqrt(own * 128)

    rows0 = jnp.stack([out_grad, hop(out_grad, dzh=1)])
    rows0 = over_x(rows0).reshape(8 * own, width)
    rows1 = hop(rows0, dc=1)

    hp = hidden_pre.reshape(NX, 2, 2, own, hid)
    hp = jnp.where(zh == 1, hp[:, ::-1], hp)
    hp = jnp.where(c == 1, hp[:, :, ::-1], hp)
    hp = lax.dynamic_slice_in_dim(jnp.concatenate([hp, hp]), x, NX, 0)
    hp = hp.transpose(2, 0, 1, 3, 4).reshape(16 * own, hid)
    value, slope = gelu_parts(hp.astype(F32))
    activation = value.astype(BF)
    act_all = lax.all_gather(activation.reshape(16, own, hid), "dp", axis=0)

    both = jnp.stack([out_grad, inputs]).reshape(2, own, 2, NY, cols)
    keep = lax.dynamic_index_in_dim(both, zl, 2, keepdims=False)
    give = lax.dynamic_index_in_dim(both, 1 - zl, 2, keepdims=False)
    both = jnp.stack([keep, hop(give, dzl=1)])
    parts = []
    for k in range(NY):
        block = lax.dynamic_index_in_dim(both, (y + k) % NY, 3, keepdims=False)
        parts.append(hop(block, dy=k) if k else block)
    parts = jnp.stack([parts[0], parts[3], parts[2], parts[1]] * 2)
    parts = lax.dynamic_slice_in_dim(parts, NY - y, NY, 0)
    parts = jnp.where(zl == 1, parts[:, ::-1], parts)
    parts = parts.transpose(2, 1, 0, 3, 4).reshape(2, 8 * own, cols)
    wide = jnp.stack([parts, hop(parts, dzh=1)])
    og0 = over_x(wide[:, 0]).reshape(64 * own, cols)
    in0 = over_x(wide[:, 1]).reshape(64 * own, cols)
    og_cols = jnp.concatenate([og0, hop(og0, dc=1)])
    in_cols = jnp.concatenate([in0, hop(in0, dc=1)])

    pre0 = (contract_last(rows0, w_out) * slope[: 8 * own]).astype(BF)
    pre1 = (contract_last(rows1, w_out) * slope[8 * own :]).astype(BF)
    pre_grad = jnp.concatenate([pre0, pre1])
    pre_all = lax.all_gather(pre_grad.reshape(16, own, hid), "dp", axis=0)

    theirs = contract_last(pre1, w_in).astype(BF)
    mine = contract_last(pre0, w_in)
    total = (mine + hop(theirs, dc=1).astype(F32)).astype(BF).reshape(NX, 2, own, width)
    near_r = hop(total[2, 0], dx=1)
    near_l = hop(total[2, 1], dx=-1)
    to_r = jnp.stack([(total[1, 0].astype(F32) + near_r.astype(F32)).astype(BF), total[1, 1]])
    to_l = jnp.stack([total[3, 0], (total[3, 1].astype(F32) + near_l.astype(F32)).astype(BF)])
    got_l = hop(to_r, dx=1)
    got_r = hop(to_l, dx=-1)
    total = total[0].astype(F32) + got_l.astype(F32) + got_r.astype(F32)
    input_grad = (total[0] + hop(total[1].astype(BF), dzh=1).astype(F32)).astype(BF)

    act_all = act_all.transpose(1, 0, 2, 3).reshape(128 * own, hid)
    out_weight_grad = contract_rows(act_all, og_cols) * scale
    pre_all = pre_all.transpose(1, 0, 2, 3).reshape(128 * own, hid)
    in_weight_grad = contract_rows(in_cols, pre_all) * scale
    return (input_grad, in_weight_grad, out_weight_grad)


def solution(mesh):
    return jax.shard_map(
        per_device,
        mesh=mesh,
        in_specs=(
            P(("dp", "mp"), None),
            P(("dp", "mp"), None),
            P("dp", "mp"),
            P(None, "mp"),
            P("mp", None),
        ),
        out_specs=(P(("dp", "mp"), None), P("dp", "mp"), P("mp", "dp")),
        check_vma=False,
    )
```

```python
import math

import jax
import jax.numpy as jnp
from jax import lax
from jax.experimental import pallas as pl
from jax.experimental.pallas import tpu as pltpu
from jax.sharding import PartitionSpec as P

root_two_pi = math.sqrt(2.0 / math.pi)
cubic_coef = 0.044715
AXES = ("dp", "mp")
NX, NY = 4, 4
BF, F32 = jnp.bfloat16, jnp.float32


def gelu_parts(pre):
    inner = root_two_pi * (pre + cubic_coef * pre * pre * pre)
    tanh_part = jnp.tanh(inner)
    value = 0.5 * pre * (1.0 + tanh_part)
    slope = 0.5 * (1.0 + tanh_part) + 0.5 * pre * (1.0 - tanh_part * tanh_part) * root_two_pi * (
        1.0 + 3.0 * cubic_coef * pre * pre
    )
    return (value, slope)


def contract_rows(left, right):
    return lax.dot_general(left, right, (((0,), (0,)), ((), ())), preferred_element_type=F32)


def contract_last(left, right):
    return lax.dot_general(left, right, (((1,), (1,)), ((), ())), preferred_element_type=F32)


def number(zl, y, x, zh, c):
    return (zl * NY + y) * 16 + x * 4 + zh * 2 + c


def hop(array, dzl=0, dy=0, dx=0, dzh=0, dc=0):
    pairs = []
    for zl in range(2):
        for y in range(NY):
            for x in range(NX):
                for zh in range(2):
                    for c in range(2):
                        there = number(zl ^ dzl, (y + dy) % NY, (x + dx) % NX, zh ^ dzh, c ^ dc)
                        pairs.append((number(zl, y, x, zh, c), there))
    return lax.ppermute(array, AXES, pairs)


def over_y(array):
    groups = [[number(zl, y, 0, 0, 0) + m for y in range(NY)] for zl in range(2) for m in range(16)]
    return lax.all_gather(array, AXES, axis=0, axis_index_groups=groups)


def over_x(array):
    groups = [[16 * g + 4 * x + m for x in range(NX)] for g in range(8) for m in range(4)]
    return lax.all_gather(array, AXES, axis=0, axis_index_groups=groups)


def after(array, *others):
    return lax.optimization_barrier((array, *others))[0]


WHOLE = pl.BlockSpec(memory_space=pltpu.VMEM)
ANY = pl.BlockSpec(memory_space=pl.ANY)
LIMIT = 56 << 20


def copy_all(pairs, sems):
    copies = [pltpu.make_async_copy(a, b, sems.at[k]) for k, (a, b) in enumerate(pairs)]
    for copy in copies:
        copy.start()
    for copy in copies:
        copy.wait()


def arranged(name, shapes, plan, sources, gates=(), held=(), vmem=()):
    n, m = len(sources) + len(held), len(gates)

    def body(*refs):
        copy_all(plan(refs[:n], refs[n + m : -1]), refs[-1])

    size = sum(math.prod(shape) for shape in shapes)
    return pl.pallas_call(
        body,
        out_shape=[pltpu.VMEM(shape, BF) if k in vmem else jax.ShapeDtypeStruct(shape, BF) for k, shape in enumerate(shapes)],
        in_specs=[WHOLE] * n + [ANY] * m,
        out_specs=[WHOLE] * len(shapes),
        scratch_shapes=[pltpu.SemaphoreType.DMA((80,))],
        cost_estimate=pl.CostEstimate(flops=0, bytes_accessed=4 * size, transcendentals=0),
        name=name,
    )(*sources, *held, *gates)


def gelu_kernel(source, act, slope, held, sems):
    mp = lax.axis_index("mp")
    x, zh, c = mp // 4, lax.rem(mp // 2, 2), lax.rem(mp, 2)
    pairs = []
    for j in range(16):
        dc, dx, dzh = j // 8, (0, 1, 3, 2)[j // 2 % 4], j % 2
        block = lax.rem(x + dx, NX) * 4 + lax.rem(zh + dzh, 2) * 2 + lax.rem(c + dc, 2)
        pairs.append((source.at[block], held.at[j]))
    copy_all(pairs, sems)

    @pl.loop(0, 16)
    def _(j):
        value, bend = gelu_parts(held[j].astype(F32))
        act[j] = value.astype(BF)
        slope[j] = bend


def gelu(hidden, gate):
    return pl.pallas_call(
        lambda source, gate, *rest: gelu_kernel(source, *rest),
        out_shape=[jax.ShapeDtypeStruct(hidden.shape, BF), jax.ShapeDtypeStruct(hidden.shape, F32)],
        in_specs=[ANY, ANY],
        out_specs=[WHOLE, WHOLE],
        scratch_shapes=[pltpu.VMEM(hidden.shape, BF), pltpu.SemaphoreType.DMA((16,))],
        compiler_params=pltpu.CompilerParams(vmem_limit_bytes=LIMIT),
        cost_estimate=pl.CostEstimate(flops=20 * hidden.size, bytes_accessed=8 * hidden.size, transcendentals=hidden.size),
        name="gelu",
    )(hidden, gate)


def pre_gradient(rows, w_out, slope, gates=()):
    n, m = len(rows), len(gates)
    half, width = rows[0].shape
    hid = w_out.shape[0]
    parts = hid // 256

    def body(*refs):
        w, bend = refs[n], refs[n + 1]
        out, w_held, sems = refs[n + 2 + m :]
        copies = []
        for k in range(parts):
            part = pl.ds(k * 256, 256)
            copies.append(pltpu.make_async_copy(w.at[part], w_held.at[part], sems.at[k]))
        for copy in copies:
            copy.start()
        for k in range(parts):
            part = pl.ds(k * 256, 256)
            copies[k].wait()
            for i in range(n):
                there = pl.ds(i * half, half)
                value = contract_last(refs[i][...], w_held[part])
                out[there, part] = (value * bend[there, part]).astype(BF)

    return pl.pallas_call(
        body,
        out_shape=jax.ShapeDtypeStruct((n * half, hid), BF),
        in_specs=[WHOLE] * n + [ANY, WHOLE] + [ANY] * m,
        out_specs=WHOLE,
        scratch_shapes=[pltpu.VMEM((hid, width), BF), pltpu.SemaphoreType.DMA((parts,))],
        compiler_params=pltpu.CompilerParams(vmem_limit_bytes=40 << 20),
        cost_estimate=pl.CostEstimate(
            flops=2 * n * half * width * hid, bytes_accessed=2 * width * (n * half + hid), transcendentals=0
        ),
        name="pre_gradient",
    )(*rows, w_out, slope, *gates)


def row_gradient(pre, first, w_in, own, gates=()):
    half, hid = pre.shape[0] // 2, pre.shape[1]
    width, step = w_in.shape[0], 512
    parts, m = width // step, len(gates)

    def body(*refs):
        pre_ref, w = refs[0], refs[1]
        out, rows, w_held, sems = refs[-4:]
        copies = [pltpu.make_async_copy(pre_ref.at[pl.ds(first, half)], rows, sems.at[parts])]
        for k in range(parts):
            part = pl.ds(k * step, step)
            copies.append(pltpu.make_async_copy(w.at[part], w_held.at[part], sems.at[k]))
        for copy in copies:
            copy.start()
        copies[0].wait()
        for k in range(parts):
            part = pl.ds(k * step, step)
            copies[1 + k].wait()
            value = contract_last(rows[...], w_held[part])
            for i in range(half // own):
                out[i, :, part] = value[i * own : (i + 1) * own].astype(BF)

    return pl.pallas_call(
        body,
        out_shape=jax.ShapeDtypeStruct((half // own, own, width), BF),
        in_specs=[ANY] * (2 + m),
        out_specs=WHOLE,
        scratch_shapes=[
            pltpu.VMEM((half, hid), BF),
            pltpu.VMEM((width, hid), BF),
            pltpu.SemaphoreType.DMA((parts + 1,)),
        ],
        compiler_params=pltpu.CompilerParams(vmem_limit_bytes=LIMIT),
        cost_estimate=pl.CostEstimate(
            flops=2 * half * width * hid, bytes_accessed=2 * width * (half + hid), transcendentals=0
        ),
        name="row_gradient",
    )(pre, w_in, *gates)


def sums(name, shapes, plan, sources, gates=(), held=()):
    n, m = len(sources), len(gates) + len(held)

    def body(*refs):
        for out, terms in plan(refs[:n], refs[n + m :]):
            total = terms[0][...].astype(F32)
            for term in terms[1:]:
                total = total + term[...].astype(F32)
            out[...] = total.astype(BF)

    size = sum(math.prod(shape) for shape in shapes)
    return pl.pallas_call(
        body,
        out_shape=[jax.ShapeDtypeStruct(shape, BF) for shape in shapes],
        in_specs=[WHOLE] * (n + len(held)) + [ANY] * len(gates),
        out_specs=[WHOLE] * len(shapes),
        cost_estimate=pl.CostEstimate(flops=2 * size, bytes_accessed=6 * size, transcendentals=0),
        name=name,
    )(*sources, *held, *gates)


def product(name, specs, sources, left_shape, right_shape, plan, scale, out_type, carry=None, gates=()):
    n, m = len(sources), len(gates)
    rows = math.prod(left_shape[:-1])
    wide_l, wide_r = left_shape[-1], right_shape[-1]

    def body(*refs):
        out, left, right, sems = refs[-4:]
        copy_all(plan(refs[:n], left, right), sems)
        for k in range(wide_l // 256):
            part = pl.ds(k * 256, 256)
            one = left[..., part].reshape(rows, 256)
            value = contract_rows(one, right[...].reshape(rows, wide_r)) * scale
            if carry is not None:
                value = value + refs[n][part].astype(F32)
            out[part] = value.astype(out.dtype)

    extra = () if carry is None else (carry,)
    return pl.pallas_call(
        body,
        out_shape=jax.ShapeDtypeStruct((wide_l, wide_r), out_type),
        in_specs=specs + [WHOLE] * len(extra) + [ANY] * m,
        out_specs=WHOLE,
        scratch_shapes=[
            pltpu.VMEM(left_shape, BF),
            pltpu.VMEM(right_shape, BF),
            pltpu.SemaphoreType.DMA((32,)),
        ],
        compiler_params=pltpu.CompilerParams(vmem_limit_bytes=LIMIT),
        cost_estimate=pl.CostEstimate(
            flops=2 * rows * wide_l * wide_r, bytes_accessed=2 * rows * (wide_l + wide_r), transcendentals=0
        ),
        name=name,
    )(*sources, *extra, *gates)


def out_part(act_all, rows, blocks, part, scale, carry=None, gates=()):
    hid = act_all.shape[2]
    half, cols = blocks[0][0].shape[0], blocks[0][0].shape[1] // 2

    def plan(refs, left, right):
        dp = lax.axis_index("dp")
        y, zl = lax.rem(dp, NY), lax.rem(dp // NY + part, 2)
        column = pl.ds(pl.multiple_of((zl * NY + y) * cols, cols), cols)
        pairs = []
        for dc in range(2):
            pairs.append((refs[1 + dc].at[:, column], right.at[dc]))
            for k in range(NY):
                source = refs[0].at[lax.rem(y + NY - k, NY), pl.ds(dc * half, half)]
                pairs.append((source, left.at[2 * k + dc]))
                if k:
                    block = refs[2 + 3 * dc + k].at[:, pl.ds(part * cols, cols)]
                    pairs.append((block, right.at[2 * k + dc]))
        return pairs

    out_type = BF if carry is None else F32
    shapes = (2 * NY, half, hid), (2 * NY, half, cols)
    sources = (act_all, *rows, *blocks[0], *blocks[1])
    specs = [ANY] * 9
    return product("out_part", specs, sources, *shapes, plan, scale, out_type, carry, gates)


def in_part(gathered, pre_all, scale, gates=()):
    small, hid = pre_all.shape[3:]
    block, cols = gathered[0].shape[1], gathered[0].shape[2] // 2

    def plan(refs, left, right):
        x = lax.axis_index("mp") // 4
        pairs = []
        for core in range(2):
            for k, dx in enumerate((0, 1, 3, 2)):
                source = refs[core].at[lax.rem(x + dx, NX)]
                for d in range(2):
                    pairs.append((source.at[:, pl.ds(d * cols, cols)], left.at[core * NX + k, d]))
        for d in range(2):
            for y in range(NY):
                pairs.append((refs[2].at[y, d], right.at[:, d * NY + y]))
        return pairs

    shapes = (2 * NX, 2, block, cols), (2 * NX, 2 * NY, small, hid)
    return product("in_part", [ANY] * 3, (*gathered, pre_all), *shapes, plan, scale, F32, None, gates)


def per_device(inputs, out_grad, hidden_pre, w_in, w_out):
    own, width = out_grad.shape
    cols = width // 8
    pair, side = 2 * cols, NY * cols
    hid = hidden_pre.shape[1]
    half = 8 * own
    scale = 1.0 / math.sqrt(own * 128)

    def place():
        dp = lax.axis_index("dp")
        return dp // NY, lax.rem(dp, NY)

    def at(offset, size):
        return pl.ds(pl.multiple_of(offset, size), size)

    gz = hop(out_grad, dzh=1)
    other_side = 1 - lax.axis_index("dp") // NY
    in_z = hop(lax.dynamic_slice_in_dim(inputs, other_side * side, side, 1), dzl=1)
    a0, b0 = hop(out_grad, dx=-1), hop(out_grad, dx=1)
    activation, slope = gelu(hidden_pre.reshape(16, own, hid), hidden_pre)
    activation, slope = activation.reshape(2 * half, hid), slope.reshape(2 * half, hid)
    act_all = over_y(activation)

    def first_plan(refs, outs):
        zl, y = place()
        pairs = []
        for k in range(NY):
            to = lax.rem(y + k, NY)
            pairs.append((refs[0].at[:, at((zl * NY + to) * cols, cols)], outs[k].at[:, pl.ds(0, cols)]))
            pairs.append((refs[1].at[:, at(to * cols, cols)], outs[k].at[:, pl.ds(cols, cols)]))
        return pairs

    blocks = arranged("first", [(own, pair)] * NY, first_plan, [inputs, in_z], [activation], [gz, a0, b0])
    parts = [hop(block, dy=k) if k else block for k, block in enumerate(blocks)]
    a1, b1 = hop(after(gz, blocks[1]), dx=-1), hop(after(gz, blocks[1]), dx=1)

    def wide_plan(refs, outs):
        zl, y = place()
        pairs = []
        for k in range(NY):
            pairs.append((refs[k].at[:, pl.ds(0, cols)], outs[0].at[lax.rem(y + NY - k, NY), :, pl.ds(0, cols)]))
            pairs.append((refs[k].at[:, pl.ds(cols, cols)], outs[0].at[lax.rem(y + NY - k, NY), :, pl.ds(cols, cols)]))
        return pairs

    (wide,) = arranged("wide", [(NY, own, pair)], wide_plan, parts, (), [a1, b1])
    wide_z = hop(wide, dzh=1)
    f0, f1 = hop(after(out_grad, wide), dx=2), hop(after(gz, wide), dx=2)

    def rows_plan(refs, outs):
        zl, y = place()
        pairs = [(refs[2 + k], outs[1].at[k]) for k in range(8)]
        pairs += [(refs[d].at[k], outs[0].at[k, d]) for k in range(NY) for d in range(2)]
        for k in range(1, NY):
            to = lax.rem(y + k, NY)
            for d in range(2):
                column = at((lax.rem(zl + d, 2) * NY + to) * cols, cols)
                for i in range(8):
                    pairs.append((refs[2 + i].at[:, column], outs[k + 1].at[i, :, pl.ds(d * cols, cols)]))
        return pairs

    shapes = [(NY, 2, own, pair), (8, own, width)] + [(8, own, pair)] * 3
    pieces = [wide, wide_z, out_grad, gz, a0, a1, b0, b1, f0, f1]
    in_, rows, *og = arranged("rows", shapes, rows_plan, pieces, [act_all], (), [1])
    rows = rows.reshape(half, width)
    rows = [rows, hop(rows, dc=1)]
    in_all = over_x(in_.reshape(half, pair))
    og = [hop(block.reshape(half, pair), dy=k + 1) for k, block in enumerate(og)]

    pre = pre_gradient(rows, w_out, slope)
    theirs = row_gradient(pre, half, w_in, own)
    pz = hop(pre, dzl=1)

    def pair_plan(refs, outs):
        return [(refs[d], outs[0].at[d]) for d in range(2)]

    (both,) = arranged("pair", [(2, *pre.shape)], pair_plan, [pre, pz], [theirs], og)
    pre_all = over_y(both).reshape(NY, 2, 8, 2 * own, hid)
    og_c = [hop(block, dc=1) for block in og]
    in_c = hop(after(in_all, both), dc=1)

    mine = row_gradient(pre, 0, w_in, own)
    theirs = hop(after(theirs, both), dc=1)
    block = (own, width)

    def cores_plan(refs, outs):
        return [(outs[k // 6].at[k] if k < 6 else outs[k - 5], [refs[0].at[k], refs[1].at[k]]) for k in range(8)]

    t, far_0, far_1 = sums("cores", [(6, *block), block, block], cores_plan, [mine, theirs])

    near_r, near_l = hop(far_0, dx=1), hop(far_1, dx=-1)

    def next_plan(refs, outs):
        s, r, l = refs
        return [
            (outs[0].at[0], [s.at[2], r]),
            (outs[0].at[1], [s.at[3]]),
            (outs[1].at[0], [s.at[4]]),
            (outs[1].at[1], [s.at[5], l]),
        ]

    out_own = out_part(act_all, rows, (og, og_c), 1, scale, None, [t])
    to_r, to_l = sums("next", [(2, *block)] * 2, next_plan, [t, near_r, near_l], [out_own])
    got_l, got_r = hop(to_r, dx=1), hop(to_l, dx=-1)


    def last_plan(refs, outs):
        return [(outs[d], [refs[0].at[d], refs[1].at[d], refs[2].at[d]]) for d in range(2)]

    keep, give = sums("last", [block] * 2, last_plan, [t, got_l, got_r])
    other = hop(give, dzh=1)

    out_far = hop(out_own, dzl=1)
    in_weight_grad = in_part((in_all, in_c), pre_all, scale)
    out_weight_grad = out_part(act_all, rows, (og, og_c), 0, scale, out_far, [in_weight_grad])
    (input_grad,) = sums("final", [block], lambda refs, outs: [(outs[0], refs)], [keep, other], [in_weight_grad])
    return (input_grad, in_weight_grad, out_weight_grad)


def solution(mesh):
    return jax.shard_map(
        per_device,
        mesh=mesh,
        in_specs=(
            P(("dp", "mp"), None),
            P(("dp", "mp"), None),
            P("dp", "mp"),
            P(None, "mp"),
            P("mp", None),
        ),
        out_specs=(P(("dp", "mp"), None), P("dp", "mp"), P("mp", "dp")),
        check_vma=False,
    )
```

```python
import math

import jax
import jax.numpy as jnp
from jax import lax
from jax.experimental import pallas as pl
from jax.experimental.pallas import tpu as pltpu
from jax.sharding import PartitionSpec as P

root_two_pi = math.sqrt(2.0 / math.pi)
cubic_coef = 0.044715
AXES = ("dp", "mp")
NX, NY = 4, 4
BF, F32 = jnp.bfloat16, jnp.float32


def gelu_parts(pre):
    inner = root_two_pi * (pre + cubic_coef * pre * pre * pre)
    tanh_part = jnp.tanh(inner)
    value = 0.5 * pre * (1.0 + tanh_part)
    slope = 0.5 * (1.0 + tanh_part) + 0.5 * pre * (1.0 - tanh_part * tanh_part) * root_two_pi * (
        1.0 + 3.0 * cubic_coef * pre * pre
    )
    return (value, slope)


def contract_rows(left, right):
    return lax.dot_general(left, right, (((0,), (0,)), ((), ())), preferred_element_type=F32)


def contract_last(left, right):
    return lax.dot_general(left, right, (((1,), (1,)), ((), ())), preferred_element_type=F32)


def number(zl, y, x, zh, c):
    return (zl * NY + y) * 16 + x * 4 + zh * 2 + c


def hop(array, dzl=0, dy=0, dx=0, dzh=0, dc=0):
    pairs = []
    for zl in range(2):
        for y in range(NY):
            for x in range(NX):
                for zh in range(2):
                    for c in range(2):
                        there = number(zl ^ dzl, (y + dy) % NY, (x + dx) % NX, zh ^ dzh, c ^ dc)
                        pairs.append((number(zl, y, x, zh, c), there))
    return lax.ppermute(array, AXES, pairs)


def over_y(array):
    groups = [[number(zl, y, 0, 0, 0) + m for y in range(NY)] for zl in range(2) for m in range(16)]
    return lax.all_gather(array, AXES, axis=0, axis_index_groups=groups)


def over_x(array):
    groups = [[16 * g + 4 * x + m for x in range(NX)] for g in range(8) for m in range(4)]
    return lax.all_gather(array, AXES, axis=0, axis_index_groups=groups)


def after(array, *others):
    return lax.optimization_barrier((array, *others))[0]


WHOLE = pl.BlockSpec(memory_space=pltpu.VMEM)
ANY = pl.BlockSpec(memory_space=pl.ANY)
LIMIT = 56 << 20


def copy_all(pairs, sems):
    copies = [pltpu.make_async_copy(a, b, sems.at[k]) for k, (a, b) in enumerate(pairs)]
    for copy in copies:
        copy.start()
    for copy in copies:
        copy.wait()


def arranged(name, shapes, plan, sources, gates=(), held=(), vmem=()):
    n, m = len(sources) + len(held), len(gates)

    def body(*refs):
        copy_all(plan(refs[:n], refs[n + m : -1]), refs[-1])

    size = sum(math.prod(shape) for shape in shapes)
    return pl.pallas_call(
        body,
        out_shape=[pltpu.VMEM(shape, BF) if k in vmem else jax.ShapeDtypeStruct(shape, BF) for k, shape in enumerate(shapes)],
        in_specs=[WHOLE] * n + [ANY] * m,
        out_specs=[WHOLE] * len(shapes),
        scratch_shapes=[pltpu.SemaphoreType.DMA((80,))],
        cost_estimate=pl.CostEstimate(flops=0, bytes_accessed=4 * size, transcendentals=0),
        name=name,
    )(*sources, *held, *gates)


def gelu_kernel(source, act, slope, held, sems):
    mp = lax.axis_index("mp")
    x, zh, c = mp // 4, lax.rem(mp // 2, 2), lax.rem(mp, 2)
    pairs = []
    for j in range(16):
        dc, dx, dzh = j // 8, (0, 1, 3, 2)[j // 2 % 4], j % 2
        block = lax.rem(x + dx, NX) * 4 + lax.rem(zh + dzh, 2) * 2 + lax.rem(c + dc, 2)
        pairs.append((source.at[block], held.at[j]))
    copy_all(pairs, sems)

    @pl.loop(0, 16)
    def _(j):
        value, bend = gelu_parts(held[j].astype(F32))
        act[j] = value.astype(BF)
        slope[j] = bend


def gelu(hidden, gate):
    return pl.pallas_call(
        lambda source, gate, *rest: gelu_kernel(source, *rest),
        out_shape=[jax.ShapeDtypeStruct(hidden.shape, BF), jax.ShapeDtypeStruct(hidden.shape, F32)],
        in_specs=[ANY, ANY],
        out_specs=[WHOLE, WHOLE],
        scratch_shapes=[pltpu.VMEM(hidden.shape, BF), pltpu.SemaphoreType.DMA((16,))],
        compiler_params=pltpu.CompilerParams(vmem_limit_bytes=LIMIT),
        cost_estimate=pl.CostEstimate(flops=20 * hidden.size, bytes_accessed=8 * hidden.size, transcendentals=hidden.size),
        name="gelu",
    )(hidden, gate)


def pre_gradient(rows, w_out, slope, gates=()):
    n, m = len(rows), len(gates)
    half, width = rows[0].shape
    hid = w_out.shape[0]
    parts = hid // 256

    def body(*refs):
        w, bend = refs[n], refs[n + 1]
        out, w_held, sems = refs[n + 2 + m :]
        copies = []
        for k in range(parts):
            part = pl.ds(k * 256, 256)
            copies.append(pltpu.make_async_copy(w.at[part], w_held.at[part], sems.at[k]))
        for copy in copies:
            copy.start()
        for k in range(parts):
            part = pl.ds(k * 256, 256)
            copies[k].wait()
            for i in range(n):
                there = pl.ds(i * half, half)
                value = contract_last(refs[i][...], w_held[part])
                out[there, part] = (value * bend[there, part]).astype(BF)

    return pl.pallas_call(
        body,
        out_shape=jax.ShapeDtypeStruct((n * half, hid), BF),
        in_specs=[WHOLE] * n + [ANY, WHOLE] + [ANY] * m,
        out_specs=WHOLE,
        scratch_shapes=[pltpu.VMEM((hid, width), BF), pltpu.SemaphoreType.DMA((parts,))],
        compiler_params=pltpu.CompilerParams(vmem_limit_bytes=40 << 20),
        cost_estimate=pl.CostEstimate(
            flops=2 * n * half * width * hid, bytes_accessed=2 * width * (n * half + hid), transcendentals=0
        ),
        name="pre_gradient",
    )(*rows, w_out, slope, *gates)


def row_gradient(pre, first, w_in, own, gates=()):
    half, hid = pre.shape[0] // 2, pre.shape[1]
    width, step = w_in.shape[0], 512
    parts, m = width // step, len(gates)

    def body(*refs):
        pre_ref, w = refs[0], refs[1]
        out, rows, w_held, sems = refs[-4:]
        copies = [pltpu.make_async_copy(pre_ref.at[pl.ds(first, half)], rows, sems.at[parts])]
        for k in range(parts):
            part = pl.ds(k * step, step)
            copies.append(pltpu.make_async_copy(w.at[part], w_held.at[part], sems.at[k]))
        for copy in copies:
            copy.start()
        copies[0].wait()
        for k in range(parts):
            part = pl.ds(k * step, step)
            copies[1 + k].wait()
            value = contract_last(rows[...], w_held[part])
            for i in range(half // own):
                out[i, :, part] = value[i * own : (i + 1) * own].astype(BF)

    return pl.pallas_call(
        body,
        out_shape=jax.ShapeDtypeStruct((half // own, own, width), BF),
        in_specs=[ANY] * (2 + m),
        out_specs=WHOLE,
        scratch_shapes=[
            pltpu.VMEM((half, hid), BF),
            pltpu.VMEM((width, hid), BF),
            pltpu.SemaphoreType.DMA((parts + 1,)),
        ],
        compiler_params=pltpu.CompilerParams(vmem_limit_bytes=LIMIT),
        cost_estimate=pl.CostEstimate(
            flops=2 * half * width * hid, bytes_accessed=2 * width * (half + hid), transcendentals=0
        ),
        name="row_gradient",
    )(pre, w_in, *gates)


def sums(name, shapes, plan, sources, gates=(), held=()):
    n, m = len(sources), len(gates) + len(held)

    def body(*refs):
        for out, terms in plan(refs[:n], refs[n + m :]):
            total = terms[0][...].astype(F32)
            for term in terms[1:]:
                total = total + term[...].astype(F32)
            out[...] = total.astype(BF)

    size = sum(math.prod(shape) for shape in shapes)
    return pl.pallas_call(
        body,
        out_shape=[jax.ShapeDtypeStruct(shape, BF) for shape in shapes],
        in_specs=[WHOLE] * (n + len(held)) + [ANY] * len(gates),
        out_specs=[WHOLE] * len(shapes),
        cost_estimate=pl.CostEstimate(flops=2 * size, bytes_accessed=6 * size, transcendentals=0),
        name=name,
    )(*sources, *held, *gates)


def product(name, specs, sources, left_shape, right_shape, plan, scale, out_type, gates=()):
    n, m = len(sources), len(gates)
    rows = math.prod(left_shape[:-1])
    wide_l, wide_r = left_shape[-1], right_shape[-1]

    def body(*refs):
        out, left, right, sems = refs[-4:]
        copy_all(plan(refs[:n], left, right), sems)
        for k in range(wide_l // 256):
            part = pl.ds(k * 256, 256)
            one = left[..., part].reshape(rows, 256)
            value = contract_rows(one, right[...].reshape(rows, wide_r)) * scale
            out[part] = value.astype(out.dtype)

    return pl.pallas_call(
        body,
        out_shape=jax.ShapeDtypeStruct((wide_l, wide_r), out_type),
        in_specs=specs + [ANY] * m,
        out_specs=WHOLE,
        scratch_shapes=[
            pltpu.VMEM(left_shape, BF),
            pltpu.VMEM(right_shape, BF),
            pltpu.SemaphoreType.DMA((32,)),
        ],
        compiler_params=pltpu.CompilerParams(vmem_limit_bytes=LIMIT),
        cost_estimate=pl.CostEstimate(
            flops=2 * rows * wide_l * wide_r, bytes_accessed=2 * rows * (wide_l + wide_r), transcendentals=0
        ),
        name=name,
    )(*sources, *gates)


def out_part(act_all, rows, blocks, part, scale, out_type, gates=()):
    hid = act_all.shape[2]
    half, cols = blocks[0][0].shape[0], blocks[0][0].shape[1] // 2

    def plan(refs, left, right):
        dp = lax.axis_index("dp")
        y, zl = lax.rem(dp, NY), lax.rem(dp // NY + part, 2)
        column = pl.ds(pl.multiple_of((zl * NY + y) * cols, cols), cols)
        pairs = []
        for dc in range(2):
            pairs.append((refs[1 + dc].at[:, column], right.at[dc]))
            for k in range(NY):
                source = refs[0].at[lax.rem(y + NY - k, NY), pl.ds(dc * half, half)]
                pairs.append((source, left.at[2 * k + dc]))
                if k:
                    block = refs[2 + 3 * dc + k].at[:, pl.ds(part * cols, cols)]
                    pairs.append((block, right.at[2 * k + dc]))
        return pairs

    shapes = (2 * NY, half, hid), (2 * NY, half, cols)
    sources = (act_all, *rows, *blocks[0], *blocks[1])
    specs = [ANY] * 9
    return product("out_part", specs, sources, *shapes, plan, scale, out_type, gates)


def in_part(gathered, pre_all, scale, gates=()):
    small, hid = pre_all.shape[3:]
    block, cols = gathered[0].shape[1], gathered[0].shape[2] // 2

    def plan(refs, left, right):
        x = lax.axis_index("mp") // 4
        pairs = []
        for core in range(2):
            for k, dx in enumerate((0, 1, 3, 2)):
                source = refs[core].at[lax.rem(x + dx, NX)]
                for d in range(2):
                    pairs.append((source.at[:, pl.ds(d * cols, cols)], left.at[core * NX + k, d]))
        for d in range(2):
            for y in range(NY):
                pairs.append((refs[2].at[y, d], right.at[:, d * NY + y]))
        return pairs

    shapes = (2 * NX, 2, block, cols), (2 * NX, 2 * NY, small, hid)
    return product("in_part", [ANY] * 3, (*gathered, pre_all), *shapes, plan, scale, F32, gates)


def per_device(inputs, out_grad, hidden_pre, w_in, w_out):
    own, width = out_grad.shape
    cols = width // 8
    pair, side = 2 * cols, NY * cols
    hid = hidden_pre.shape[1]
    half = 8 * own
    scale = 1.0 / math.sqrt(own * 128)

    def place():
        dp = lax.axis_index("dp")
        return dp // NY, lax.rem(dp, NY)

    def at(offset, size):
        return pl.ds(pl.multiple_of(offset, size), size)

    gz = hop(out_grad, dzh=1)
    other_side = 1 - lax.axis_index("dp") // NY
    in_z = hop(lax.dynamic_slice_in_dim(inputs, other_side * side, side, 1), dzl=1)
    a0, b0 = hop(out_grad, dx=-1), hop(out_grad, dx=1)
    def first_plan(refs, outs):
        zl, y = place()
        pairs = []
        for k in range(NY):
            to = lax.rem(y + k, NY)
            pairs.append((refs[0].at[:, at((zl * NY + to) * cols, cols)], outs[k].at[:, pl.ds(0, cols)]))
            pairs.append((refs[1].at[:, at(to * cols, cols)], outs[k].at[:, pl.ds(cols, cols)]))
        return pairs

    blocks = arranged("first", [(own, pair)] * NY, first_plan, [inputs, in_z], [], [gz, a0, b0])
    parts = [hop(block, dy=k) if k else block for k, block in enumerate(blocks)]
    a1, b1 = hop(after(gz, blocks[1]), dx=-1), hop(after(gz, blocks[1]), dx=1)

    activation, slope = gelu(hidden_pre.reshape(16, own, hid), blocks[1])
    activation, slope = activation.reshape(2 * half, hid), slope.reshape(2 * half, hid)
    act_all = over_y(activation)

    def wide_plan(refs, outs):
        zl, y = place()
        pairs = []
        for k in range(NY):
            pairs.append((refs[k].at[:, pl.ds(0, cols)], outs[0].at[lax.rem(y + NY - k, NY), :, pl.ds(0, cols)]))
            pairs.append((refs[k].at[:, pl.ds(cols, cols)], outs[0].at[lax.rem(y + NY - k, NY), :, pl.ds(cols, cols)]))
        return pairs

    (wide,) = arranged("wide", [(NY, own, pair)], wide_plan, parts, [activation], [a1, b1])
    wide_z = hop(wide, dzh=1)
    f0, f1 = hop(after(out_grad, wide), dx=2), hop(after(gz, wide), dx=2)

    def rows_plan(refs, outs):
        zl, y = place()
        pairs = [(refs[2 + k], outs[1].at[k]) for k in range(8)]
        pairs += [(refs[d].at[k], outs[0].at[k, d]) for k in range(NY) for d in range(2)]
        for k in range(1, NY):
            to = lax.rem(y + k, NY)
            for d in range(2):
                column = at((lax.rem(zl + d, 2) * NY + to) * cols, cols)
                for i in range(8):
                    pairs.append((refs[2 + i].at[:, column], outs[k + 1].at[i, :, pl.ds(d * cols, cols)]))
        return pairs

    shapes = [(NY, 2, own, pair), (8, own, width)] + [(8, own, pair)] * 3
    pieces = [wide, wide_z, out_grad, gz, a0, a1, b0, b1, f0, f1]
    in_, rows, *og = arranged("rows", shapes, rows_plan, pieces, (), (), [1])
    rows = rows.reshape(half, width)
    rows = [rows, hop(rows, dc=1)]
    in_all = over_x(in_.reshape(half, pair))
    og = [hop(block.reshape(half, pair), dy=k + 1) for k, block in enumerate(og)]

    pre = pre_gradient(rows, w_out, slope)
    theirs = row_gradient(pre, half, w_in, own)
    pz = hop(pre, dzl=1)

    both = jnp.stack([after(pre, theirs, act_all, *og), pz])
    pre_all = over_y(both).reshape(NY, 2, 8, 2 * own, hid)
    og_c = [hop(block, dc=1) for block in og]
    in_c = hop(after(in_all, both), dc=1)

    mine = row_gradient(pre, 0, w_in, own)
    theirs = hop(after(theirs, both), dc=1)
    block = (own, width)

    def cores_plan(refs, outs):
        return [(outs[k // 6].at[k] if k < 6 else outs[k - 5], [refs[0].at[k], refs[1].at[k]]) for k in range(8)]

    t, far_0, far_1 = sums("cores", [(6, *block), block, block], cores_plan, [mine, theirs])

    near_r, near_l = hop(far_0, dx=1), hop(far_1, dx=-1)

    def next_plan(refs, outs):
        s, r, l = refs
        return [
            (outs[0].at[0], [s.at[2], r]),
            (outs[0].at[1], [s.at[3]]),
            (outs[1].at[0], [s.at[4]]),
            (outs[1].at[1], [s.at[5], l]),
        ]

    out_own = out_part(act_all, rows, (og, og_c), 1, scale, BF, [t])
    to_r, to_l = sums("next", [(2, *block)] * 2, next_plan, [t, near_r, near_l], [out_own])
    got_l, got_r = hop(to_r, dx=1), hop(to_l, dx=-1)


    def last_plan(refs, outs):
        return [(outs[d], [refs[0].at[d], refs[1].at[d], refs[2].at[d]]) for d in range(2)]

    out_near = out_part(act_all, rows, (og, og_c), 0, scale, F32, [to_r])
    keep, give = sums("last", [block] * 2, last_plan, [t, got_l, got_r], [out_near])
    other = hop(give, dzh=1)

    out_far = hop(out_own, dzl=1)
    in_weight_grad = in_part((in_all, in_c), pre_all, scale)
    out_weight_grad = out_near + after(out_far, in_weight_grad).astype(F32)
    (input_grad,) = sums("final", [block], lambda refs, outs: [(outs[0], refs)], [keep, other], [in_weight_grad])
    return (input_grad, in_weight_grad, out_weight_grad)


def solution(mesh):
    return jax.shard_map(
        per_device,
        mesh=mesh,
        in_specs=(
            P(("dp", "mp"), None),
            P(("dp", "mp"), None),
            P("dp", "mp"),
            P(None, "mp"),
            P("mp", None),
        ),
        out_specs=(P(("dp", "mp"), None), P("dp", "mp"), P("mp", "dp")),
        check_vma=False,
    )
```
